32 devices in a mesh: rep: 2 (over x), gx: 8 (over z, y), gy: 2 (over core).
Axes of the slice: x: 2, y: 2, z: 4, core: 2. Of those that a mesh axis runs over, the one named last changes fastest.
Arguments:
- gate_pre: bfloat16 [2048, 26624], P('rep', ('gx', 'gy')), parts along dimension 0, may hold values from -6 to 6
- up_pre: bfloat16 [2048, 26624], P('rep', ('gx', 'gy')), parts along dimension 0, may hold values from -6 to 6
- down_weight: bfloat16 [26624, 8192], P('gx', 'gy'), may hold values from -0.0546875 to 0.0546875
Outputs:
- layer_out: bfloat16 [2048, 8192], P('rep', ('gy', 'gx')), parts along dimension 0
The draws below stay inside these ranges and needn't reach their ends.
There are 2 independent parts, one for each index of `rep`. The reference program is written for one: setup_inputs(seed, part) draws one part's arguments, and reference() takes and returns one part's arrays. A program takes and returns all parts, laid end to end along the dimension named above; an argument that names none is the same for every part. Nothing has to cross between parts.
All inputs are finite; a program needn't handle non-finite values.
Results may differ from the reference program's by a relative error of at most 0.0049.
Values may be sent and summed in bfloat16 or wider, within the bound.
A program may use at most 128 MiB of HBM per device.

```python
import jax
import jax.numpy as jnp

D = 8192
FF = 26624
BATCH = 1024


def raised(array, stream_key, source, target, parts, factor):
    owner, partner = [(jnp.arange(array.shape[dim]) // (array.shape[dim] // parts)).reshape([-1 if axis == dim else 1 for axis in range(array.ndim)]) for dim in (source, target)]
    chosen = jax.random.permutation(stream_key, parts)[partner]
    strong = (owner == chosen) | (owner == (partner + parts // 2) % parts)
    return jnp.where(strong, factor * array, array)


def shard_levels(key, dims, pieces, least, high):
    gain = 1.0
    for dim, blocks in pieces:
        draws = jax.random.uniform(jax.random.fold_in(jax.random.fold_in(key, 6), dim), (blocks,), jnp.float32, least / len(pieces), high / len(pieces))
        gain = gain * jnp.repeat(jnp.exp(draws), dims[dim] // blocks).reshape((-1,) + (1,) * (len(dims) - 1 - dim))
    return gain


def gaussian(key, dims, deviation, bound, split=(), dtype=jnp.bfloat16):
    gain = shard_levels(key, dims, split, -0.22, 0.18) if split else 1.0
    result = jax.random.normal(key, dims, jnp.float32) * deviation * gain
    return jnp.minimum(jnp.maximum(result, -bound), bound).astype(dtype)


def gaussian_with(rng, extent, width, bound, pieces, heavy, held_as=jnp.bfloat16):
    result = width * jax.random.normal(rng, extent, jnp.float32)
    if pieces:
        result = result * shard_levels(rng, extent, pieces, -0.22, 0.18)
    return jnp.clip(raised(result, jax.random.fold_in(rng, 3), *heavy), -bound, bound).astype(held_as)


def setup_inputs(seed: int = 0, part: int = 0) -> dict:
    arg_keys = jax.random.split(jax.random.key(seed), 4)
    part_keys = jax.random.split(jax.random.fold_in(arg_keys[3], part), 4)
    return {
        "gate_pre": gaussian(part_keys[0], (BATCH, FF), 1.0, 6.0, ((1, 16),)),
        "up_pre": gaussian(part_keys[1], (BATCH, FF), 1.0, 6.0, ((1, 16),)),
        "down_weight": gaussian_with(arg_keys[2], (FF, D), FF ** -0.5, 0.0546875, ((0, 8), (1, 2)), (0, 1, 8, 2.0)),
    }


def reference(gate_pre, up_pre, down_weight):
    gate = gate_pre.astype(jnp.float32)
    hidden = (jax.nn.silu(gate) * up_pre.astype(jnp.float32)).astype(jnp.bfloat16)
    return jnp.dot(hidden, down_weight, preferred_element_type=jnp.float32).astype(jnp.bfloat16)
```

```python
import functools

import jax
import jax.numpy as jnp
from jax import lax
from jax.experimental import pallas as pl
from jax.experimental.pallas import tpu as pltpu
from jax.sharding import PartitionSpec as P

MESH = pl.DeviceIdType.MESH
WSLOTS = 3
F32 = jnp.float32
BF16 = jnp.bfloat16


def activate(gate_vals, up_vals):
    return (jax.nn.silu(gate_vals.astype(F32)) * up_vals.astype(F32)).astype(BF16)


def plain_shards(gate_pre, up_pre, down_weight):
    hidden = lax.all_gather(activate(gate_pre, up_pre), "gy", axis=1, tiled=True)
    partial_out = jnp.dot(hidden, down_weight, preferred_element_type=F32)
    return lax.psum_scatter(partial_out, "gx", scatter_dimension=1, tiled=True).astype(BF16)


def kernel(
    gate_ref, up_ref, w_ref, out_ref,
    gbuf, ubuf, hid, wbuf, part, ybuf, zlo, zup,
    gsem, usem, wsem, h_send, h_recv,
    y_send, y_recv, up_send, dn_send, zlo_recv, zup_recv,
):
    rows, half = gate_ref.shape
    cols = out_ref.shape[1]
    step = rows // 4
    ch = rows // 8
    core = lax.axis_index("gy")
    g = lax.axis_index("gx")
    z = g // 2
    y = g % 2
    low = z < 2
    end = jnp.logical_or(z == 0, z == 3)
    mid = jnp.logical_not(end)
    ypeer = z * 2 + (1 - y)
    upward = jnp.where(low, g + 2, g - 2)
    downward = jnp.where(low, g - 2, g + 2)

    def owner(i):
        k = jnp.where(end, (3, 2, 1, 0)[i // 2], (3, 0, 2, 1)[i // 2])
        zz = jnp.where(low, k, 3 - k)
        return zz * 2 + (1 - y if i % 2 == 0 else y)

    def load_in(r):
        at = pl.ds(r * step, step)
        return (
            pltpu.make_async_copy(gate_ref.at[at], gbuf.at[at], gsem.at[r]),
            pltpu.make_async_copy(up_ref.at[at], ubuf.at[at], usem.at[r]),
        )

    def load_w(i):
        s = i % WSLOTS
        c = pl.ds(pl.multiple_of(owner(i) * cols, cols), cols)
        mine = pl.ds(pl.multiple_of(core * half, half), half)
        other = pl.ds(pl.multiple_of((1 - core) * half, half), half)
        return (
            pltpu.make_async_copy(w_ref.at[mine, c], wbuf.at[s, pl.ds(0, half)], wsem.at[s, 0]),
            pltpu.make_async_copy(w_ref.at[other, c], wbuf.at[s, pl.ds(half, half)], wsem.at[s, 1]),
        )

    def start(copies):
        for copy in copies:
            copy.start()

    def wait(copies):
        for copy in copies:
            copy.wait()

    def exchange(r):
        at = pl.ds(r * step, step)
        return pltpu.make_async_remote_copy(
            src_ref=hid.at[at, pl.ds(0, half)], dst_ref=hid.at[at, pl.ds(half, half)],
            send_sem=h_send.at[r], recv_sem=h_recv.at[r],
            device_id={"gy": 1 - core}, device_id_type=MESH,
        )

    def chunk(i, n):
        return part.at[i, pl.ds(pl.multiple_of(n * ch, ch), ch)]

    def to_y(i, n, s):
        return pltpu.make_async_remote_copy(
            src_ref=chunk(i, n), dst_ref=ybuf.at[s], send_sem=y_send.at[s], recv_sem=y_recv.at[s],
            device_id={"gx": ypeer}, device_id_type=MESH,
        )

    def end_up(i, n, s):
        return pltpu.make_async_remote_copy(
            src_ref=chunk(i, n), dst_ref=zlo.at[s], send_sem=up_send.at[s], recv_sem=zlo_recv.at[s],
            device_id={"gx": upward}, device_id_type=MESH,
        )

    def mid_up(i, n, s):
        return pltpu.make_async_remote_copy(
            src_ref=chunk(i, n), dst_ref=zup.at[s], send_sem=up_send.at[s], recv_sem=zup_recv.at[s],
            device_id={"gx": upward}, device_id_type=MESH,
        )

    def mid_down(i, n, s):
        return pltpu.make_async_remote_copy(
            src_ref=chunk(i, n), dst_ref=zup.at[s], send_sem=dn_send.at[s], recv_sem=zup_recv.at[s],
            device_id={"gx": downward}, device_id_type=MESH,
        )

    def act(r):
        wait(load_in(r))

        @pl.loop(0, step // 16)
        def _(t):
            at = pl.ds(pl.multiple_of(r * step + t * 16, 16), 16)
            v = gbuf[at, :].astype(F32)
            h = (0.5 * v) * (jnp.tanh(0.5 * v) + 1.0)
            hid[at, pl.ds(0, half)] = (h * ubuf[at, :].astype(F32)).astype(BF16)

    def mm(i, r):
        at = pl.ds(r * step, step) if isinstance(r, int) else pl.ds(pl.multiple_of(r * step, step), step)
        part[i, at, :] = jnp.dot(
            hid[at, :], wbuf[i % WSLOTS], preferred_element_type=F32
        ).astype(BF16)

    def got_y(s):
        to_y(0, 0, s).wait_recv()
        return ybuf[s].astype(F32)

    def got_lo(s):
        end_up(0, 0, s).wait_recv()
        return zlo[s].astype(F32)

    def got_up(s):
        mid_up(0, 0, s).wait_recv()
        return zup[s].astype(F32)

    def total(i, n, *terms):
        at = pl.ds(pl.multiple_of(n * ch, ch), ch)
        value = part[i, at, :].astype(F32)
        for term in terms:
            value = value + term
        return value.astype(BF16)

    def add(i, n, *terms):
        at = pl.ds(pl.multiple_of(n * ch, ch), ch)
        part[i, at, :] = total(i, n, *terms)

    def final(i, n, *terms):
        at = pl.ds(pl.multiple_of(n * ch, ch), ch)
        out_ref[at, :] = total(i, n, *terms)

    def each(count, body):
        pl.loop(0, count)(body)

    for r in range(4):
        start(load_in(r))
    for i in range(WSLOTS):
        start(load_w(i))
    barrier = pltpu.get_barrier_semaphore()
    pl.semaphore_signal(barrier, inc=1, device_id={"gy": 1 - core}, device_id_type=MESH)
    pl.semaphore_signal(barrier, inc=1, device_id={"gx": ypeer}, device_id_type=MESH)
    pl.semaphore_signal(barrier, inc=1, device_id={"gx": upward}, device_id_type=MESH)

    @pl.when(mid)
    def _():
        pl.semaphore_signal(barrier, inc=1, device_id={"gx": downward}, device_id_type=MESH)

    act(0)
    pl.semaphore_wait(barrier, 3 + mid.astype(jnp.int32))
    exchange(0).start()
    act(1)
    exchange(1).start()

    for r in range(4):
        exchange(r).wait_recv()
        if r == 0:
            wait(load_w(0))
        mm(0, r)
        to_y(0, 2 * r + 1, r).start()

        @pl.when(end)
        def _():
            end_up(0, 2 * r, r).start()

        if r == 0:
            wait(load_w(1))
        mm(1, r)

        @pl.when(end)
        def _():
            end_up(1, 2 * r, 4 + r).start()

        if r < 2:
            act(r + 2)
            exchange(r + 2).start()
    start(load_w(3))
    start(load_w(4))

    def block(i):
        wait(load_w(i))
        each(4, lambda r: mm(i, r))
        if i >= 2 and i + WSLOTS < 8:
            start(load_w(i + WSLOTS))

    block(2)

    @pl.when(end)
    def _():
        each(8, lambda n: to_y(2, n, 4 + n).start())

    @pl.when(mid)
    def _():
        each(4, lambda n: to_y(2, 2 * n + 1, 20 + n).start())

    block(3)

    @pl.when(end)
    def _():
        def o3b(n):
            add(1, 2 * n + 1, got_y(n))
            end_up(1, 2 * n + 1, 8 + n).start()

        each(4, o3b)

    @pl.when(mid)
    def _():
        def x3a(n):
            add(0, 2 * n, got_lo(n))
            mid_up(0, 2 * n, n).start()

        each(4, x3a)

        def x0a(n):
            add(2, 2 * n, got_up(n))
            mid_down(2, 2 * n, n).start()

        each(4, x0a)

    block(4)

    @pl.when(end)
    def _():
        each(8, lambda n: to_y(4, n, 12 + n).start())

    @pl.when(mid)
    def _():
        each(8, lambda n: to_y(4, n, 4 + n).start())

    block(5)

    @pl.when(mid)
    def _():
        def o3a(n):
            add(1, 2 * n, got_lo(4 + n))
            mid_up(1, 2 * n, 4 + n).start()

        each(4, o3a)

        def o0a(n):
            add(3, 2 * n, got_up(4 + n))
            mid_down(3, 2 * n, 4 + n).start()

        each(4, o0a)

    block(6)

    @pl.when(end)
    def _():
        each(4, lambda n: to_y(6, 2 * n + 1, 20 + n).start())

    @pl.when(mid)
    def _():
        each(8, lambda n: to_y(6, n, 12 + n).start())

    block(7)

    @pl.when(end)
    def _():
        def o2(n):
            add(3, n, got_y(4 + n))
            end_up(3, n, 12 + n).start()

        each(8, o2)

        def x0a(n):
            add(6, 2 * n, got_up(n))
            to_y(6, 2 * n, 24 + n).start()

        each(4, x0a)

        def o1(n):
            add(5, n, got_y(12 + n))
            end_up(5, n, 20 + n).start()

        each(8, o1)
        each(4, lambda n: final(7, 2 * n + 1, got_y(20 + n), got_up(8 + n)))
        each(4, lambda n: final(7, 2 * n, got_y(24 + n), got_up(4 + n)))

    @pl.when(mid)
    def _():
        def ends(n):
            add(1, 2 * n + 1, got_y(n), got_lo(8 + n))
            mid_up(1, 2 * n + 1, 8 + n).start()
            add(3, 2 * n + 1, got_y(20 + n), got_up(8 + n))
            mid_down(3, 2 * n + 1, 8 + n).start()

        each(4, ends)

        def o2(n):
            add(5, n, got_y(4 + n), got_lo(12 + n))
            mid_up(5, n, 12 + n).start()

        each(8, o2)
        each(8, lambda n: final(7, n, got_y(12 + n), got_lo(20 + n), got_up(12 + n)))

    for r in range(4):
        exchange(r).wait_send()

    each(24, lambda s: to_y(0, 0, s).wait_send())

    @pl.when(end)
    def _():
        each(4, lambda s: to_y(0, 0, 24 + s).wait_send())
        each(28, lambda s: end_up(0, 0, s).wait_send())

    @pl.when(mid)
    def _():
        each(20, lambda s: mid_up(0, 0, s).wait_send())
        each(12, lambda s: mid_down(0, 0, s).wait_send())


def fused_shards(gate_pre, up_pre, down_weight):
    rows, half = gate_pre.shape
    depth, width = down_weight.shape
    cols = width // 8
    ch = rows // 8
    dma = pltpu.SemaphoreType.DMA
    return pl.pallas_call(
        kernel,
        out_shape=jax.ShapeDtypeStruct((rows, cols), BF16),
        in_specs=[pl.BlockSpec(memory_space=pl.ANY)] * 3,
        out_specs=pl.BlockSpec(memory_space=pltpu.VMEM),
        scratch_shapes=[
            pltpu.VMEM((rows, half), BF16),
            pltpu.VMEM((rows, half), BF16),
            pltpu.VMEM((rows, depth), BF16),
            pltpu.VMEM((WSLOTS, depth, cols), BF16),
            pltpu.VMEM((8, rows, cols), BF16),
            pltpu.VMEM((28, ch, cols), BF16),
            pltpu.VMEM((28, ch, cols), BF16),
            pltpu.VMEM((20, ch, cols), BF16),
            dma((4,)), dma((4,)), dma((WSLOTS, 2)), dma((4,)), dma((4,)),
            dma((28,)), dma((28,)), dma((28,)), dma((12,)), dma((28,)), dma((20,)),
        ],
        compiler_params=pltpu.CompilerParams(
            collective_id=0, has_side_effects=True, vmem_limit_bytes=60 * 1024 * 1024
        ),
        cost_estimate=pl.CostEstimate(
            flops=2 * rows * depth * width,
            bytes_accessed=2 * (depth * width + 2 * rows * half + rows * cols),
            transcendentals=rows * half,
        ),
    )(gate_pre, up_pre, down_weight)


def solution(mesh):
    placed = (P("rep", ("gx", "gy")), P("rep", ("gx", "gy")), P("gx", "gy"))
    fits = mesh.shape["gx"] == 8 and mesh.shape["gy"] == 2
    return jax.shard_map(
        fused_shards if fits else plain_shards,
        mesh=mesh, in_specs=placed, out_specs=P("rep", ("gy", "gx")), check_vma=False,
    )
```

```python
import functools

import jax
import jax.numpy as jnp
from jax import lax
from jax.experimental import pallas as pl
from jax.experimental.pallas import tpu as pltpu
from jax.sharding import PartitionSpec as P

MESH = pl.DeviceIdType.MESH
WSLOTS = 6
F32 = jnp.float32
BF16 = jnp.bfloat16


def activate(gate_vals, up_vals):
    return (jax.nn.silu(gate_vals.astype(F32)) * up_vals.astype(F32)).astype(BF16)


def plain_shards(gate_pre, up_pre, down_weight):
    hidden = lax.all_gather(activate(gate_pre, up_pre), "gy", axis=1, tiled=True)
    partial_out = jnp.dot(hidden, down_weight, preferred_element_type=F32)
    return lax.psum_scatter(partial_out, "gx", scatter_dimension=1, tiled=True).astype(BF16)


def kernel(
    gate_ref, up_ref, w_ref, out_ref,
    gbuf, ubuf, hid, wbuf, part, ybuf, zlo, zup,
    gsem, usem, wsem, h_send, h_recv,
    y_send, y_recv, up_send, dn_send, zlo_recv, zup_recv,
):
    rows, half = gate_ref.shape
    cols = out_ref.shape[1]
    step = rows // 4
    ch = rows // 8
    core = lax.axis_index("gy")
    g = lax.axis_index("gx")
    z = g // 2
    y = g % 2
    low = z < 2
    end = jnp.logical_or(z == 0, z == 3)
    mid = jnp.logical_not(end)
    ypeer = z * 2 + (1 - y)
    upward = jnp.where(low, g + 2, g - 2)
    downward = jnp.where(low, g - 2, g + 2)

    def owner(i):
        k = jnp.where(end, (3, 2, 1, 0)[i // 2], (3, 0, 2, 1)[i // 2])
        zz = jnp.where(low, k, 3 - k)
        return zz * 2 + (1 - y if i % 2 == 0 else y)

    def load_in(r):
        at = pl.ds(r * step, step)
        return (
            pltpu.make_async_copy(gate_ref.at[at], gbuf.at[at], gsem.at[r]),
            pltpu.make_async_copy(up_ref.at[at], ubuf.at[at], usem.at[r]),
        )

    def load_w(i):
        s = i % WSLOTS
        c = pl.ds(pl.multiple_of(owner(i) * cols, cols), cols)
        mine = pl.ds(pl.multiple_of(core * half, half), half)
        other = pl.ds(pl.multiple_of((1 - core) * half, half), half)
        return (
            pltpu.make_async_copy(w_ref.at[mine, c], wbuf.at[s, pl.ds(0, half)], wsem.at[s, 0]),
            pltpu.make_async_copy(w_ref.at[other, c], wbuf.at[s, pl.ds(half, half)], wsem.at[s, 1]),
        )

    def start(copies):
        for copy in copies:
            copy.start()

    def wait(copies):
        for copy in copies:
            copy.wait()

    def exchange(n):
        at = pl.ds(n * ch, ch)
        return pltpu.make_async_remote_copy(
            src_ref=hid.at[at, pl.ds(0, half)], dst_ref=hid.at[at, pl.ds(half, half)],
            send_sem=h_send.at[n], recv_sem=h_recv.at[n],
            device_id={"gy": 1 - core}, device_id_type=MESH,
        )

    def chunk(i, n):
        return part.at[i, pl.ds(pl.multiple_of(n * ch, ch), ch)]

    def to_y(i, n, s):
        return pltpu.make_async_remote_copy(
            src_ref=chunk(i, n), dst_ref=ybuf.at[s], send_sem=y_send.at[s], recv_sem=y_recv.at[s],
            device_id={"gx": ypeer}, device_id_type=MESH,
        )

    def end_up(i, n, s):
        return pltpu.make_async_remote_copy(
            src_ref=chunk(i, n), dst_ref=zlo.at[s], send_sem=up_send.at[s], recv_sem=zlo_recv.at[s],
            device_id={"gx": upward}, device_id_type=MESH,
        )

    def mid_up(i, n, s):
        return pltpu.make_async_remote_copy(
            src_ref=chunk(i, n), dst_ref=zup.at[s], send_sem=up_send.at[s], recv_sem=zup_recv.at[s],
            device_id={"gx": upward}, device_id_type=MESH,
        )

    def mid_down(i, n, s):
        return pltpu.make_async_remote_copy(
            src_ref=chunk(i, n), dst_ref=zup.at[s], send_sem=dn_send.at[s], recv_sem=zup_recv.at[s],
            device_id={"gx": downward}, device_id_type=MESH,
        )

    def act(n):
        if n % 2 == 0:
            wait(load_in(n // 2))

        @pl.loop(0, ch // 16)
        def _(t):
            at = pl.ds(pl.multiple_of(n * ch + t * 16, 16), 16)
            v = gbuf[at, :].astype(F32)
            h = (0.5 * v) * (jnp.tanh(0.5 * v) + 1.0)
            hid[at, pl.ds(0, half)] = (h * ubuf[at, :].astype(F32)).astype(BF16)

    def mm(i, r):
        at = pl.ds(r * step, step) if isinstance(r, int) else pl.ds(pl.multiple_of(r * step, step), step)
        part[i, at, :] = jnp.dot(
            hid[at, :], wbuf[i % WSLOTS], preferred_element_type=F32
        ).astype(BF16)

    def got_y(s):
        to_y(0, 0, s).wait_recv()
        return ybuf[s].astype(F32)

    def got_lo(s):
        end_up(0, 0, s).wait_recv()
        return zlo[s].astype(F32)

    def got_up(s):
        mid_up(0, 0, s).wait_recv()
        return zup[s].astype(F32)

    def total(i, n, *terms):
        at = pl.ds(pl.multiple_of(n * ch, ch), ch)
        value = part[i, at, :].astype(F32)
        for term in terms:
            value = value + term
        return value.astype(BF16)

    def add(i, n, *terms):
        at = pl.ds(pl.multiple_of(n * ch, ch), ch)
        part[i, at, :] = total(i, n, *terms)

    def final(i, n, *terms):
        at = pl.ds(pl.multiple_of(n * ch, ch), ch)
        out_ref[at, :] = total(i, n, *terms)

    def each(count, body):
        pl.loop(0, count)(body)

    for r in range(4):
        start(load_in(r))
    barrier = pltpu.get_barrier_semaphore()
    pl.semaphore_signal(barrier, inc=1, device_id={"gy": 1 - core}, device_id_type=MESH)
    pl.semaphore_signal(barrier, inc=1, device_id={"gx": ypeer}, device_id_type=MESH)
    pl.semaphore_signal(barrier, inc=1, device_id={"gx": upward}, device_id_type=MESH)

    @pl.when(mid)
    def _():
        pl.semaphore_signal(barrier, inc=1, device_id={"gx": downward}, device_id_type=MESH)

    act(0)
    pl.semaphore_wait(barrier, 3 + mid.astype(jnp.int32))
    exchange(0).start()
    start(load_w(0))
    for n in range(1, 8):
        act(n)
        exchange(n).start()
        if n < WSLOTS:
            start(load_w(n))

    def end_merge(r):
        add(1, 2 * r + 1, got_y(r))
        end_up(1, 2 * r + 1, 8 + r).start()
        for n in (2 * r, 2 * r + 1):
            add(3, n, got_y(4 + n))
            end_up(3, n, 12 + n).start()

    def up_pair(r):
        add(0, 2 * r, got_lo(r))
        mid_up(0, 2 * r, r).start()
        add(1, 2 * r, got_lo(4 + r))
        mid_up(1, 2 * r, 4 + r).start()

    def down_pair(r):
        add(2, 2 * r, got_up(r))
        mid_down(2, 2 * r, r).start()
        add(3, 2 * r, got_up(4 + r))
        mid_down(3, 2 * r, 4 + r).start()

    for r in range(4):
        exchange(2 * r).wait_recv()
        exchange(2 * r + 1).wait_recv()
        if r == 0:
            wait(load_w(0))
        mm(0, r)
        to_y(0, 2 * r + 1, r).start()

        @pl.when(end)
        def _():
            end_up(0, 2 * r, r).start()

        if r == 0:
            wait(load_w(1))
        mm(1, r)

        @pl.when(end)
        def _():
            end_up(1, 2 * r, 4 + r).start()

        if r == 0:
            wait(load_w(2))
        mm(2, r)

        @pl.when(end)
        def _():
            to_y(2, 2 * r, 4 + 2 * r).start()
            to_y(2, 2 * r + 1, 5 + 2 * r).start()

        @pl.when(mid)
        def _():
            to_y(2, 2 * r + 1, 20 + r).start()

        if r == 0:
            wait(load_w(3))
        mm(3, r)
    start(load_w(6))
    start(load_w(7))

    def block(i):
        wait(load_w(i))
        each(4, lambda r: mm(i, r))

    block(4)

    @pl.when(end)
    def _():
        each(8, lambda n: to_y(4, n, 12 + n).start())

    @pl.when(mid)
    def _():
        each(8, lambda n: to_y(4, n, 4 + n).start())
        each(2, up_pair)

    block(5)

    @pl.when(end)
    def _():
        each(2, end_merge)

    @pl.when(mid)
    def _():
        each(2, down_pair)
        up_pair(2)

    block(6)

    @pl.when(end)
    def _():
        each(4, lambda n: to_y(6, 2 * n + 1, 20 + n).start())
        end_merge(2)

    @pl.when(mid)
    def _():
        each(8, lambda n: to_y(6, n, 12 + n).start())
        up_pair(3)
        down_pair(2)

    block(7)

    @pl.when(end)
    def _():
        end_merge(3)

        def x0a(n):
            add(6, 2 * n, got_up(n))
            to_y(6, 2 * n, 24 + n).start()

        each(4, x0a)

        def o1(n):
            add(5, n, got_y(12 + n))
            end_up(5, n, 20 + n).start()

        each(8, o1)
        each(4, lambda n: final(7, 2 * n + 1, got_y(20 + n), got_up(8 + n)))
        each(4, lambda n: final(7, 2 * n, got_y(24 + n), got_up(4 + n)))

    @pl.when(mid)
    def _():
        down_pair(3)

        def merge(r):
            add(1, 2 * r + 1, got_y(r), got_lo(8 + r))
            mid_up(1, 2 * r + 1, 8 + r).start()
            for n in (2 * r, 2 * r + 1):
                add(5, n, got_y(4 + n), got_lo(12 + n))
                mid_up(5, n, 12 + n).start()
            add(3, 2 * r + 1, got_y(20 + r), got_up(8 + r))
            mid_down(3, 2 * r + 1, 8 + r).start()

        each(4, merge)
        each(8, lambda n: final(7, n, got_y(12 + n), got_lo(20 + n), got_up(12 + n)))

    for n in range(8):
        exchange(n).wait_send()

    each(24, lambda s: to_y(0, 0, s).wait_send())

    @pl.when(end)
    def _():
        each(4, lambda s: to_y(0, 0, 24 + s).wait_send())
        each(28, lambda s: end_up(0, 0, s).wait_send())

    @pl.when(mid)
    def _():
        each(20, lambda s: mid_up(0, 0, s).wait_send())
        each(12, lambda s: mid_down(0, 0, s).wait_send())


def fused_shards(gate_pre, up_pre, down_weight):
    rows, half = gate_pre.shape
    depth, width = down_weight.shape
    cols = width // 8
    ch = rows // 8
    dma = pltpu.SemaphoreType.DMA
    return pl.pallas_call(
        kernel,
        out_shape=jax.ShapeDtypeStruct((rows, cols), BF16),
        in_specs=[pl.BlockSpec(memory_space=pl.ANY)] * 3,
        out_specs=pl.BlockSpec(memory_space=pltpu.VMEM),
        scratch_shapes=[
            pltpu.VMEM((rows, half), BF16),
            pltpu.VMEM((rows, half), BF16),
            pltpu.VMEM((rows, depth), BF16),
            pltpu.VMEM((WSLOTS, depth, cols), BF16),
            pltpu.VMEM((8, rows, cols), BF16),
            pltpu.VMEM((28, ch, cols), BF16),
            pltpu.VMEM((28, ch, cols), BF16),
            pltpu.VMEM((20, ch, cols), BF16),
            dma((4,)), dma((4,)), dma((WSLOTS, 2)), dma((8,)), dma((8,)),
            dma((28,)), dma((28,)), dma((28,)), dma((12,)), dma((28,)), dma((20,)),
        ],
        compiler_params=pltpu.CompilerParams(
            collective_id=0, has_side_effects=True, vmem_limit_bytes=60 * 1024 * 1024
        ),
        cost_estimate=pl.CostEstimate(
            flops=2 * rows * depth * width,
            bytes_accessed=2 * (depth * width + 2 * rows * half + rows * cols),
            transcendentals=rows * half,
        ),
    )(gate_pre, up_pre, down_weight)


def solution(mesh):
    placed = (P("rep", ("gx", "gy")), P("rep", ("gx", "gy")), P("gx", "gy"))
    fits = mesh.shape["gx"] == 8 and mesh.shape["gy"] == 2
    return jax.shard_map(
        fused_shards if fits else plain_shards,
        mesh=mesh, in_specs=placed, out_specs=P("rep", ("gy", "gx")), check_vma=False,
    )
```
